32 devices in a mesh: seq: 16 (over z, y, x), mp: 2 (over core).
Axes of the slice: x: 2, y: 2, z: 4, core: 2. Of those that a mesh axis runs over, the one named last changes fastest.
Arguments:
- byte_state: bfloat16 [16384, 1024], P('seq'), may hold values from -6 to 6
- patch_id: int32 [16384], P('seq'), may hold values from 0 to 3583, as said below
- w_query: bfloat16 [1024, 1024], P('seq', 'mp'), may hold values from -0.1875 to 0.1875
- w_key: bfloat16 [1024, 1024], P('seq', 'mp'), may hold values from -0.1875 to 0.1875
- w_value: bfloat16 [1024, 1024], P('seq', 'mp'), may hold values from -0.1875 to 0.1875
- w_out: bfloat16 [1024, 4096], P('seq', 'mp'), may hold values from -0.1875 to 0.1875
- out_grad: bfloat16 [3584, 4096], P('seq', 'mp'), may hold values from -6 to 6
Outputs:
- patch_embed: bfloat16 [3584, 4096], P('seq', 'mp')
- byte_grad: bfloat16 [16384, 1024], P('seq')
- grad_query: float32 [1024, 1024], P('seq', 'mp')
- grad_key: float32 [1024, 1024], P('seq', 'mp')
- grad_value: float32 [1024, 1024], P('seq', 'mp')
- grad_out: float32 [1024, 4096], P('seq', 'mp')
The draws below stay inside these ranges and needn't reach their ends.
Inputs may be any that keep to these rules, and one draw needn't show every extreme that they name: `patch_id`: never falls along the bytes; every patch has 1 to 16 bytes, all on one index of seq, and the first patch on each index has exactly 16. The first patch of the bytes of index s is numbered 224 * s plus an offset of 1 to 56; the offset is 0 on index 0 and 56 on some index; the last index ends with patch 3584 - 1.
All inputs are finite; a program needn't handle non-finite values.
Results may differ from the reference program's by a relative error of at most 0.002.
The reference program's roundings to bfloat16 on the way (of `pooled`, `query_proj`, `prob_half`, `attended`, `head_grad`, `value_grad`, `score_grad` and `pooled_grad`) count: a program that leaves them out, or rounds other values in their place, can miss the bound.
Values may be sent and summed in bfloat16 or wider, within the bound.
A program may use at most 128 MiB of HBM per device.

```python
import jax
import jax.numpy as jnp
from jax import lax

DL = 1024
DG = 4096
XHEADS = 16
MAXLEN = 16
BYTE_DEV = 1024
HEAD = 64
PATCH_DEV = 224
DRIFT = 56
BYTES = 16384
PATCHES = 3584
N_SEQ = 16
N_MP = 2


def patch_numbers(key):
    key = jax.random.fold_in(key, 7)
    key_drift, key_pick, key_rank = jax.random.split(key, 3)
    device = jnp.arange(N_SEQ, dtype=jnp.int32)
    drift = jax.random.randint(key_drift, (N_SEQ,), 1, DRIFT + 1)
    chosen = jax.random.randint(key_pick, (), 0, N_SEQ - 1)
    drift = jnp.where(device == chosen, DRIFT, drift)
    drift = jnp.where(device == N_SEQ - 1, 0, drift)
    before = jnp.concatenate([jnp.zeros((1,), jnp.int32), drift[:-1]])
    counts = PATCH_DEV + drift - before
    offset = device * PATCH_DEV + before
    position = jnp.arange(BYTE_DEV, dtype=jnp.int32)
    forced = (position % MAXLEN == 0) & (position > 0)
    candidate = (position % MAXLEN != 0) & (position >= MAXLEN)
    noise = jax.random.randint(key_rank, (N_SEQ, BYTE_DEV), 0, 1 << 18)
    score = jnp.where(candidate[None, :], noise * BYTE_DEV + position[None, :], (1 << 18) * BYTE_DEV + position[None, :])
    order = jnp.argsort(score, axis=1, stable=True)
    rank = jnp.argsort(order, axis=1, stable=True)
    extra = counts - BYTE_DEV // MAXLEN
    cut = forced[None, :] | candidate[None, :] & (rank < extra[:, None])
    local_index = jnp.cumsum(cut.astype(jnp.int32), axis=1)
    return (offset[:, None] + local_index).reshape(-1).astype(jnp.int32)


def projection_draw(key, tilt):
    key = jax.random.fold_in(key, tilt)
    limit = 6.0 * DL ** (-0.5)
    base = jax.random.normal(key, (DL, DL), jnp.float32) * DL ** (-0.5)
    base = jnp.clip(base, -limit, limit)
    return jnp.clip(base, -limit, limit)


def draw_patch_id(key, part):
    return patch_numbers(key)


def draw_byte_state(key, part):
    key = jax.random.fold_in(key, 3)
    key_noise = jax.random.fold_in(key, 0)
    noise = jax.random.normal(key_noise, (BYTES, DL), jnp.float32)
    state = noise
    return jnp.clip(state, -6.0, 6.0).astype(jnp.bfloat16)


def draw_w_query(key, part):
    return projection_draw(key, 5).astype(jnp.bfloat16)


def draw_w_key(key, part):
    return projection_draw(key, 9).astype(jnp.bfloat16)


def block_levels(own_key, extent, shards, smallest, high):
    loudness, own = 1.0, jax.random.fold_in(own_key, 6)
    for axis_at, blocks in shards:
        draws = jnp.exp(jax.random.uniform(jax.random.fold_in(own, axis_at), (blocks,), jnp.float32, smallest / len(shards), high / len(shards)))
        loudness = loudness * jnp.repeat(draws, extent[axis_at] // blocks).reshape([-1 if axis == axis_at else 1 for axis in range(len(extent))])
    return loudness


def gaussian(stream_key, shape, scale, reach, shards=(), kind=jnp.bfloat16):
    values = jax.random.normal(stream_key, shape, jnp.float32) * scale
    if len(shards) > 0:
        values = block_levels(stream_key, shape, shards, -0.22, 0.18) * values
    return jnp.clip(values, min=-reach, max=reach).astype(kind)


def setup_inputs(seed: int = 0) -> dict:
    seeds = jax.random.split(jax.random.key(seed), 8)
    byte_state = draw_byte_state(jax.random.fold_in(seeds[7], 71), 0)
    patch_id = draw_patch_id(jax.random.fold_in(seeds[7], 71), 0)
    w_query = draw_w_query(jax.random.fold_in(seeds[7], 71), 0)
    w_key = draw_w_key(jax.random.fold_in(seeds[7], 71), 0)
    w_value = gaussian(seeds[4], (DL, DL), DL ** -0.5, 0.1875, ((0, 16), (1, 2)))
    w_out = gaussian(seeds[5], (DL, DG), DL ** -0.5, 0.1875, ((0, 16), (1, 2)))
    out_grad = gaussian(seeds[6], (PATCHES, DG), 1.0, 6.0, ((0, 16), (1, 2)))
    return {"byte_state": byte_state, "patch_id": patch_id, "w_query": w_query, "w_key": w_key, "w_value": w_value, "w_out": w_out, "out_grad": out_grad}


def contract_cols(left_side, right_side):
    return lax.dot_general(left_side, right_side, (((1,), (1,)), ((), ())), preferred_element_type=jnp.float32)


def contract_rows(left_side, right_side):
    return lax.dot_general(left_side, right_side, (((0,), (0,)), ((), ())), preferred_element_type=jnp.float32)


def forward_group(query_proj, keys, values, flat_index, inside, col_start):
    width_cols = DL // N_MP
    group_heads = XHEADS // N_MP
    heads_query = query_proj[:, col_start:col_start + width_cols].astype(jnp.float32).reshape(PATCHES, group_heads, HEAD)
    heads_key = keys[flat_index, col_start:col_start + width_cols].astype(jnp.float32).reshape(PATCHES, MAXLEN, group_heads, HEAD)
    heads_value = values[flat_index, col_start:col_start + width_cols].astype(jnp.float32).reshape(PATCHES, MAXLEN, group_heads, HEAD)
    scores = jnp.einsum("phd,pjhd->phj", heads_query, heads_key) * (HEAD ** -0.5)
    masked = jnp.where(inside[:, None, :], scores, -1e30)
    peak = jnp.max(masked, axis=2, keepdims=True)
    exp_terms = jnp.where(inside[:, None, :], jnp.exp(masked - peak), 0.0)
    prob_float = exp_terms / jnp.sum(exp_terms, axis=2, keepdims=True)
    prob_half = lax.optimization_barrier(prob_float.astype(jnp.bfloat16)).astype(jnp.float32)
    return heads_query, heads_key, heads_value, prob_float, prob_half


def reference(byte_state, patch_id, w_query, w_key, w_value, w_out, out_grad):
    width_cols = DL // N_MP
    grad_cols = DG // N_MP
    score_scale = HEAD ** -0.5
    byte_count = jax.ops.segment_sum(jnp.ones((BYTES,), jnp.int32), patch_id, num_segments=PATCHES)
    first_byte = (jnp.cumsum(byte_count) - byte_count).astype(jnp.int32)
    count_float = byte_count.astype(jnp.float32)
    pooled = (jax.ops.segment_sum(byte_state.astype(jnp.float32), patch_id, num_segments=PATCHES) / count_float[:, None]).astype(jnp.bfloat16)
    query_proj = jnp.dot(pooled, w_query, preferred_element_type=jnp.float32).astype(jnp.bfloat16)
    keys = jnp.dot(byte_state, w_key, preferred_element_type=jnp.float32).astype(jnp.bfloat16)
    values = jnp.dot(byte_state, w_value, preferred_element_type=jnp.float32).astype(jnp.bfloat16)
    offsets = jnp.arange(MAXLEN, dtype=jnp.int32)
    window = jnp.minimum(first_byte[:, None] + offsets[None, :], BYTES - 1).astype(jnp.int32)
    inside = offsets[None, :] < byte_count[:, None]
    flat_index = window.reshape(-1)
    pieces = []
    for group_index in range(N_MP):
        parts = forward_group(query_proj, keys, values, flat_index, inside, group_index * width_cols)
        group_out = jnp.einsum("phj,pjhd->phd", parts[4], parts[2]).reshape(PATCHES, width_cols)
        pieces.append(group_out.astype(jnp.bfloat16))
    attended = jnp.concatenate(pieces, axis=1)
    patch_embed = jnp.dot(attended, w_out, preferred_element_type=jnp.float32).astype(jnp.bfloat16)
    head_sum = jnp.zeros((PATCHES, DL), jnp.float32)
    for group_index in range(N_MP):
        col_start = group_index * grad_cols
        term = contract_cols(out_grad[:, col_start:col_start + grad_cols], w_out[:, col_start:col_start + grad_cols])
        head_sum = head_sum + lax.optimization_barrier(term.astype(jnp.bfloat16)).astype(jnp.float32)
    head_grad = head_sum.astype(jnp.bfloat16)
    grad_out = contract_rows(attended, out_grad)
    byte_sum = jnp.zeros((BYTES, DL), jnp.float32)
    query_grads = []
    key_grads = []
    value_grads = []
    for group_index in range(N_MP):
        col_start = group_index * width_cols
        heads_query, heads_key, heads_value, prob_float, prob_half = forward_group(query_proj, keys, values, flat_index, inside, col_start)
        group_heads = XHEADS // N_MP
        slot_grad = head_grad[:, col_start:col_start + width_cols].astype(jnp.float32).reshape(PATCHES, group_heads, HEAD)
        prob_grad = jnp.einsum("phd,pjhd->phj", slot_grad, heads_value)
        value_pair = jnp.einsum("phj,phd->pjhd", prob_half, slot_grad).reshape(PATCHES * MAXLEN, width_cols)
        value_grad = jax.ops.segment_sum(value_pair, flat_index, num_segments=BYTES).astype(jnp.bfloat16)
        score_grad = prob_float * (prob_grad - jnp.sum(prob_float * prob_grad, axis=2, keepdims=True)) * score_scale
        score_half = lax.optimization_barrier(score_grad.astype(jnp.bfloat16)).astype(jnp.float32)
        query_grad = jnp.einsum("phj,pjhd->phd", score_half, heads_key).reshape(PATCHES, width_cols).astype(jnp.bfloat16)
        key_pair = jnp.einsum("phj,phd->pjhd", score_half, heads_query).reshape(PATCHES * MAXLEN, width_cols)
        key_grad = jax.ops.segment_sum(key_pair, flat_index, num_segments=BYTES).astype(jnp.bfloat16)
        query_grads.append(contract_rows(pooled, query_grad))
        key_grads.append(contract_rows(byte_state, key_grad))
        value_grads.append(contract_rows(byte_state, value_grad))
        pooled_grad = (contract_cols(query_grad, w_query[:, col_start:col_start + width_cols]) / count_float[:, None]).astype(jnp.bfloat16)
        group_part = contract_cols(key_grad, w_key[:, col_start:col_start + width_cols])
        group_part = group_part + contract_cols(value_grad, w_value[:, col_start:col_start + width_cols])
        group_part = group_part + pooled_grad[patch_id].astype(jnp.float32)
        byte_sum = byte_sum + lax.optimization_barrier(group_part.astype(jnp.bfloat16)).astype(jnp.float32)
    byte_grad = byte_sum.astype(jnp.bfloat16)
    return (patch_embed, byte_grad, jnp.concatenate(query_grads, axis=1), jnp.concatenate(key_grads, axis=1), jnp.concatenate(value_grads, axis=1), grad_out)
```

```python
import jax
import jax.numpy as jnp
from jax import lax
from jax.experimental import pallas as pl
from jax.experimental.pallas import tpu as pltpu
from jax.sharding import PartitionSpec as P

HEAD = 64
DRIFT = 56
MAXLEN = 16
SCALE = HEAD ** (-0.5)
VMEM_LIMIT = 48 * 1024 * 1024


def passed_along(value, axis, steps):
    count = lax.axis_size(axis)
    initial, last = (max(0, -steps), min(count, count - steps))
    return lax.ppermute(value, axis, [(source, source + steps) for source in range(initial, last)])


def swapped(value, axis, bit):
    count = lax.axis_size(axis)
    return lax.ppermute(value, axis, [(i, i ^ (1 << bit)) for i in range(count)])


def contract_cols(left_side, right_side):
    return lax.dot_general(
        left_side, right_side, (((1,), (1,)), ((), ())), preferred_element_type=jnp.float32
    )


def contract_rows(left_side, right_side):
    return lax.dot_general(
        left_side, right_side, (((0,), (0,)), ((), ())), preferred_element_type=jnp.float32
    )


def bit_order(axis, flip):
    bits = lax.axis_size(axis).bit_length() - 1
    order = list(range(bits))
    if flip and bits > 1:
        order[0], order[1] = 1, 0
    return order


def scatter_sum(value, axis, flip):
    count = lax.axis_size(axis)
    rank = lax.axis_index(axis)
    order = bit_order(axis, flip)
    bits = len(order)
    value = value.reshape((2,) * bits + (value.shape[0] // count, value.shape[1]))
    left = list(range(bits - 1, -1, -1))
    for bit in order:
        at = left.index(bit)
        mine = (rank >> bit) & 1
        send = lax.dynamic_index_in_dim(value, 1 - mine, at, keepdims=False)
        keep = lax.dynamic_index_in_dim(value, mine, at, keepdims=False)
        value = keep + swapped(send, axis, bit)
        left.pop(at)
    return value


def gather_rows(value, axis, flip):
    rank = lax.axis_index(axis)
    cols = value.shape[1]
    held = []
    for bit in reversed(bit_order(axis, flip)):
        other = swapped(value, axis, bit)
        mine = ((rank >> bit) & 1) == 0
        at = sum(1 for b in held if b > bit)
        value = jnp.stack([jnp.where(mine, value, other), jnp.where(mine, other, value)], axis=at)
        held.append(bit)
    return value.reshape(-1, cols)


def pair_sum(value, axis):
    if lax.axis_size(axis) != 2:
        return lax.psum(value, axis)
    other = swapped(value, axis, 0)
    return (value.astype(jnp.float32) + other.astype(jnp.float32)).astype(value.dtype)


def split_halves(product):
    high = product.astype(jnp.bfloat16)
    low = (product - high.astype(jnp.float32)).astype(jnp.bfloat16)
    return high, low


def neighbours(ids):
    pairs = []
    count = ids.shape[1]
    where_at = lax.broadcasted_iota(jnp.int32, ids.shape, 1)
    step = 1
    while step < MAXLEN:
        before = (pltpu.roll(ids, step, 1) == ids) & (where_at >= step)
        after = (pltpu.roll(ids, count - step, 1) == ids) & (where_at < count - step)
        pairs.append((step, before, after))
        step *= 2
    return pairs


def over_patch(value, pairs, combine, neutral):
    count = value.shape[1]
    ahead = behind = value
    for step, before, after in pairs:
        ahead = combine(ahead, jnp.where(before, pltpu.roll(ahead, step, 1), neutral))
        behind = combine(behind, jnp.where(after, pltpu.roll(behind, count - step, 1), neutral))
    return ahead, behind


def head_rows(heads, width):
    row = lax.broadcasted_iota(jnp.int32, (heads, width), 0)
    col = lax.broadcasted_iota(jnp.int32, (heads, width), 1)
    return ((col >= row * HEAD) & (col < row * HEAD + HEAD)).astype(jnp.float32).astype(jnp.bfloat16)


def forward_kernel(ids_ref, member_ref, query_ref, key_ref, value_ref, prob_ref, attended_ref):
    heads, width = prob_ref.shape[0], query_ref.shape[1]
    member = member_ref[...]
    expand = head_rows(heads, width)
    query_bytes = contract_rows(member, query_ref[...])
    high, low = split_halves(query_bytes * key_ref[...].astype(jnp.float32))
    scores = (contract_cols(expand, high) + contract_cols(expand, low)) * SCALE
    pairs = neighbours(jnp.broadcast_to(ids_ref[...], scores.shape))
    peak = jnp.maximum(*over_patch(scores, pairs, jnp.maximum, -1e30))
    terms = jnp.exp(scores - peak)
    ahead, behind = over_patch(terms, pairs, jnp.add, 0.0)
    prob = terms / (ahead + (behind - terms))
    prob_ref[...] = prob
    weight = contract_rows(prob.astype(jnp.bfloat16), expand)
    high, low = split_halves(weight * value_ref[...].astype(jnp.float32))
    attended = jnp.dot(member, high, preferred_element_type=jnp.float32) + jnp.dot(
        member, low, preferred_element_type=jnp.float32
    )
    attended_ref[...] = attended.astype(jnp.bfloat16)


def backward_kernel(
    ids_ref, member_ref, query_ref, key_ref, value_ref, prob_ref, grad_ref,
    key_grad_ref, value_grad_ref, query_grad_ref,
):
    heads, width = prob_ref.shape[0], query_ref.shape[1]
    member = member_ref[...]
    expand = head_rows(heads, width)
    prob = prob_ref[...]
    grad_bytes = contract_rows(member, grad_ref[...])
    high, low = split_halves(grad_bytes * value_ref[...].astype(jnp.float32))
    prob_grad = contract_cols(expand, high) + contract_cols(expand, low)
    value_weight = contract_rows(prob.astype(jnp.bfloat16), expand)
    value_grad_ref[...] = (value_weight * grad_bytes).astype(jnp.bfloat16)
    pairs = neighbours(jnp.broadcast_to(ids_ref[...], prob.shape))
    both = prob * prob_grad
    ahead, behind = over_patch(both, pairs, jnp.add, 0.0)
    score_grad = prob * (prob_grad - (ahead + (behind - both))) * SCALE
    weight = contract_rows(score_grad.astype(jnp.bfloat16), expand)
    query_bytes = contract_rows(member, query_ref[...])
    key_grad_ref[...] = (weight * query_bytes).astype(jnp.bfloat16)
    high, low = split_halves(weight * key_ref[...].astype(jnp.float32))
    query_grad = jnp.dot(member, high, preferred_element_type=jnp.float32) + jnp.dot(
        member, low, preferred_element_type=jnp.float32
    )
    query_grad_ref[...] = query_grad.astype(jnp.bfloat16)


def run_kernel(body, outs, *operands):
    vmem = pl.BlockSpec(memory_space=pltpu.VMEM)
    return pl.pallas_call(
        body,
        out_shape=outs,
        in_specs=[vmem] * len(operands),
        out_specs=[vmem] * len(outs),
        compiler_params=pltpu.CompilerParams(vmem_limit_bytes=VMEM_LIMIT),
        cost_estimate=pl.CostEstimate(
            flops=8_000_000_000, bytes_accessed=8_000_000, transcendentals=0
        ),
    )(*operands)


def local(byte_state, patch_id, w_query, w_key, w_value, w_out, out_grad):
    seq_rank = lax.axis_index("seq")
    model_rank = lax.axis_index("mp")
    n_model = lax.axis_size("mp")
    width = w_query.shape[1]
    half = width // 2
    heads = width // HEAD
    patch_rows = out_grad.shape[0]
    byte_rows = byte_state.shape[0]
    slots = -(-(patch_rows + DRIFT) // 128) * 128

    full_out = lax.all_gather(w_out, "seq", axis=0, tiled=True)
    first = gather_rows(jnp.concatenate([w_key, w_query[:, :half]], axis=1), "seq", False)
    second = gather_rows(jnp.concatenate([w_value, w_query[:, half:]], axis=1), "seq", True)
    full_key, full_value = first[:, :width], second[:, :width]
    full_query = jnp.concatenate([first[:, width:], second[:, width:]], axis=1)

    first_patch = patch_id[0]
    last_patch = patch_id[byte_rows - 1]
    slot_index = jnp.arange(slots, dtype=jnp.int32)
    ids = (patch_id - first_patch)[None, :]
    member = ids == slot_index[:, None]
    member_half = member.astype(jnp.bfloat16)
    length = jnp.maximum(jnp.sum(member.astype(jnp.float32), axis=1), 1.0)
    pooled = (
        jnp.dot(member_half, byte_state, preferred_element_type=jnp.float32) / length[:, None]
    ).astype(jnp.bfloat16)

    keys = jnp.dot(byte_state, full_key, preferred_element_type=jnp.float32).astype(jnp.bfloat16)
    values = jnp.dot(byte_state, full_value, preferred_element_type=jnp.float32).astype(
        jnp.bfloat16
    )
    query_proj = jnp.dot(pooled, full_query, preferred_element_type=jnp.float32).astype(
        jnp.bfloat16
    )
    prob, attended = run_kernel(
        forward_kernel,
        [
            jax.ShapeDtypeStruct((heads, byte_rows), jnp.float32),
            jax.ShapeDtypeStruct((slots, width), jnp.bfloat16),
        ],
        ids, member_half, query_proj, keys, values,
    )

    target_row = first_patch - seq_rank * patch_rows + slot_index
    slot_live = slot_index <= last_patch - first_patch
    own_map = (
        (target_row[None, :] == jnp.arange(patch_rows, dtype=jnp.int32)[:, None])
        & slot_live[None, :]
    ).astype(jnp.bfloat16)
    next_map = (
        (target_row[None, :] - patch_rows == jnp.arange(DRIFT, dtype=jnp.int32)[:, None])
        & slot_live[None, :]
    ).astype(jnp.bfloat16)
    outgoing = jnp.dot(next_map, attended, preferred_element_type=jnp.float32).astype(jnp.bfloat16)
    incoming = passed_along(outgoing, "seq", 1)
    own_block = jnp.dot(own_map, attended, preferred_element_type=jnp.float32)
    own_block = (
        own_block + jnp.pad(incoming.astype(jnp.float32), ((0, patch_rows - DRIFT), (0, 0)))
    ).astype(jnp.bfloat16)
    if n_model == 2:
        other_block = swapped(own_block, "mp", 0)
        heads_all = jnp.concatenate(
            [
                jnp.where(model_rank == 0, own_block, other_block),
                jnp.where(model_rank == 0, other_block, own_block),
            ],
            axis=1,
        )
    else:
        heads_all = lax.all_gather(own_block, "mp", axis=1, tiled=True)
    grad_out = contract_rows(heads_all, out_grad)
    out_half = grad_out.shape[1] // 2
    grad_out = jnp.concatenate(
        [
            scatter_sum(grad_out[:, :out_half], "seq", False),
            scatter_sum(grad_out[:, out_half:], "seq", True),
        ],
        axis=1,
    )
    patch_embed = jnp.dot(heads_all, full_out, preferred_element_type=jnp.float32).astype(
        jnp.bfloat16
    )

    partial_sum = contract_cols(out_grad, full_out).astype(jnp.bfloat16)
    if n_model == 2:
        mine = lax.dynamic_slice_in_dim(partial_sum, model_rank * width, width, 1)
        theirs = lax.dynamic_slice_in_dim(partial_sum, (1 - model_rank) * width, width, 1)
        head_grad = (
            mine.astype(jnp.float32) + swapped(theirs, "mp", 0).astype(jnp.float32)
        ).astype(jnp.bfloat16)
    else:
        head_grad = lax.dynamic_slice_in_dim(
            lax.psum(partial_sum, "mp"), model_rank * width, width, 1
        )
    returned = passed_along(head_grad[:DRIFT], "seq", -1)
    slot_grad = (contract_rows(own_map, head_grad) + contract_rows(next_map, returned)).astype(
        jnp.bfloat16
    )
    key_grad, value_grad, query_grad = run_kernel(
        backward_kernel,
        [
            jax.ShapeDtypeStruct((byte_rows, width), jnp.bfloat16),
            jax.ShapeDtypeStruct((byte_rows, width), jnp.bfloat16),
            jax.ShapeDtypeStruct((slots, width), jnp.bfloat16),
        ],
        ids, member_half, query_proj, keys, values, prob, slot_grad,
    )
    grad_key = scatter_sum(contract_rows(byte_state, key_grad), "seq", False)
    grad_value = scatter_sum(contract_rows(byte_state, value_grad), "seq", True)
    grad_query = contract_rows(pooled, query_grad)
    grad_query = jnp.concatenate(
        [
            scatter_sum(grad_query[:, :half], "seq", False),
            scatter_sum(grad_query[:, half:], "seq", True),
        ],
        axis=1,
    )
    pooled_grad = (contract_cols(query_grad, full_query) / length[:, None]).astype(jnp.bfloat16)
    byte_part = (
        contract_cols(key_grad, full_key)
        + contract_cols(value_grad, full_value)
        + contract_rows(member_half, pooled_grad)
    )
    byte_grad = pair_sum(byte_part.astype(jnp.bfloat16), "mp")
    return (patch_embed, byte_grad, grad_query, grad_key, grad_value, grad_out)


def solution(mesh):
    in_specs = (
        P("seq", None),
        P("seq"),
        P("seq", "mp"),
        P("seq", "mp"),
        P("seq", "mp"),
        P("seq", "mp"),
        P("seq", "mp"),
    )
    out_specs = (
        P("seq", "mp"),
        P("seq", None),
        P("seq", "mp"),
        P("seq", "mp"),
        P("seq", "mp"),
        P("seq", "mp"),
    )
    return jax.shard_map(local, mesh=mesh, in_specs=in_specs, out_specs=out_specs, check_vma=False)
```

```python
import jax
import jax.numpy as jnp
from jax import lax
from jax.experimental import pallas as pl
from jax.experimental.pallas import tpu as pltpu
from jax.sharding import PartitionSpec as P

HEAD = 64
DRIFT = 56
MAXLEN = 16
SCALE = HEAD ** (-0.5)
VMEM_LIMIT = 48 * 1024 * 1024


def passed_along(value, axis, steps):
    count = lax.axis_size(axis)
    initial, last = (max(0, -steps), min(count, count - steps))
    return lax.ppermute(value, axis, [(source, source + steps) for source in range(initial, last)])


def swapped(value, axis, bit):
    count = lax.axis_size(axis)
    return lax.ppermute(value, axis, [(i, i ^ (1 << bit)) for i in range(count)])


def contract_cols(left_side, right_side):
    return lax.dot_general(
        left_side, right_side, (((1,), (1,)), ((), ())), preferred_element_type=jnp.float32
    )


def contract_rows(left_side, right_side):
    return lax.dot_general(
        left_side, right_side, (((0,), (0,)), ((), ())), preferred_element_type=jnp.float32
    )


def bit_order(axis, flip, start=0):
    bits = lax.axis_size(axis).bit_length() - 1
    order = list(range(start, bits))
    if flip and len(order) > 1:
        order[0], order[1] = order[1], order[0]
    return order


def after(value, earlier):
    return lax.optimization_barrier((value, earlier))[0]


def scatter_sum(value, axis, flip, start=0):
    rank = lax.axis_index(axis)
    order = bit_order(axis, flip, start)
    bits = len(order)
    value = value.reshape((2,) * bits + (value.shape[0] >> bits, value.shape[1]))
    left = sorted(order, reverse=True)
    for bit in order:
        at = left.index(bit)
        mine = (rank >> bit) & 1
        send = lax.dynamic_index_in_dim(value, 1 - mine, at, keepdims=False)
        keep = lax.dynamic_index_in_dim(value, mine, at, keepdims=False)
        other = swapped(send, axis, bit)
        value = keep + other
        left.pop(at)
    return value


def gather_rows(value, axis, flip, order=None):
    rank = lax.axis_index(axis)
    cols = value.shape[1]
    held = []
    for bit in reversed(bit_order(axis, flip)) if order is None else order:
        other = swapped(value, axis, bit)
        mine = ((rank >> bit) & 1) == 0
        at = sum(1 for b in held if b > bit)
        value = jnp.stack([jnp.where(mine, value, other), jnp.where(mine, other, value)], axis=at)
        held.append(bit)
    return value.reshape(-1, cols)


def gather_pair(value, axis, held, bit):
    rank = lax.axis_index(axis)
    other = swapped(value, axis, bit)
    mine = ((rank >> bit) & 1) == 0
    at = 1 if held > bit else 0
    value = jnp.stack([jnp.where(mine, value, other), jnp.where(mine, other, value)], axis=at)
    return value.reshape(-1, value.shape[-1])


def grouped_columns(value, axis, group):
    width = value.shape[1]
    count = lax.axis_size(axis)
    block = width // count
    source = lax.broadcasted_iota(jnp.int32, (width, width), 0)
    place = lax.broadcasted_iota(jnp.int32, (width, width), 1)
    owner = (place % (width >> group)) // block << group
    for bit in range(group):
        owner = owner + ((place // (width >> (bit + 1))) % 2 << bit)
    chosen = (source == owner * block + place % block).astype(jnp.bfloat16)
    return jnp.dot(value, chosen, preferred_element_type=jnp.float32).astype(value.dtype)


def grouped_rows(value, axis, group):
    rank = lax.axis_index(axis)
    cols = value.shape[1]
    value = value[None]
    for bit in range(group):
        cols //= 2
        upper = ((rank >> bit) & 1) == 1
        low, high = value[:, :, :cols], value[:, :, cols:]
        keep, send = jnp.where(upper, high, low), jnp.where(upper, low, high)
        other = swapped(send, axis, bit)
        value = jnp.concatenate(
            [jnp.where(upper, other, keep), jnp.where(upper, keep, other)], axis=0
        )
    return value.reshape(-1, cols)


def pair_sum(value, axis):
    if lax.axis_size(axis) != 2:
        return lax.psum(value, axis)
    other = swapped(value, axis, 0)
    return (value.astype(jnp.float32) + other.astype(jnp.float32)).astype(value.dtype)


def split_halves(product):
    high = product.astype(jnp.bfloat16)
    low = (product - high.astype(jnp.float32)).astype(jnp.bfloat16)
    return high, low


def neighbours(ids):
    pairs = []
    count = ids.shape[1]
    where_at = lax.broadcasted_iota(jnp.int32, ids.shape, 1)
    step = 1
    while step < MAXLEN:
        before = (pltpu.roll(ids, step, 1) == ids) & (where_at >= step)
        after = (pltpu.roll(ids, count - step, 1) == ids) & (where_at < count - step)
        pairs.append((step, before, after))
        step *= 2
    return pairs


def over_patch(value, pairs, combine, neutral):
    count = value.shape[1]
    ahead = behind = value
    for step, before, after in pairs:
        ahead = combine(ahead, jnp.where(before, pltpu.roll(ahead, step, 1), neutral))
        behind = combine(behind, jnp.where(after, pltpu.roll(behind, count - step, 1), neutral))
    return ahead, behind


def head_rows(heads, width):
    row = lax.broadcasted_iota(jnp.int32, (heads, width), 0)
    col = lax.broadcasted_iota(jnp.int32, (heads, width), 1)
    return ((col >= row * HEAD) & (col < row * HEAD + HEAD)).astype(jnp.float32).astype(jnp.bfloat16)


def forward_kernel(ids_ref, member_ref, query_ref, key_ref, value_ref, prob_ref, attended_ref):
    heads, width = prob_ref.shape[0], query_ref.shape[1]
    member = member_ref[...]
    expand = head_rows(heads, width)
    query_bytes = contract_rows(member, query_ref[...])
    high, low = split_halves(query_bytes * key_ref[...].astype(jnp.float32))
    scores = (contract_cols(expand, high) + contract_cols(expand, low)) * SCALE
    pairs = neighbours(jnp.broadcast_to(ids_ref[...], scores.shape))
    peak = jnp.maximum(*over_patch(scores, pairs, jnp.maximum, -1e30))
    terms = jnp.exp(scores - peak)
    ahead, behind = over_patch(terms, pairs, jnp.add, 0.0)
    prob = terms / (ahead + (behind - terms))
    prob_ref[...] = prob
    weight = contract_rows(prob.astype(jnp.bfloat16), expand)
    high, low = split_halves(weight * value_ref[...].astype(jnp.float32))
    attended = jnp.dot(member, high, preferred_element_type=jnp.float32) + jnp.dot(
        member, low, preferred_element_type=jnp.float32
    )
    attended_ref[...] = attended.astype(jnp.bfloat16)


def backward_kernel(
    ids_ref, member_ref, query_ref, key_ref, value_ref, prob_ref, grad_ref,
    key_grad_ref, value_grad_ref, query_grad_ref,
):
    heads, width = prob_ref.shape[0], query_ref.shape[1]
    member = member_ref[...]
    expand = head_rows(heads, width)
    prob = prob_ref[...]
    grad_bytes = contract_rows(member, grad_ref[...])
    high, low = split_halves(grad_bytes * value_ref[...].astype(jnp.float32))
    prob_grad = contract_cols(expand, high) + contract_cols(expand, low)
    value_weight = contract_rows(prob.astype(jnp.bfloat16), expand)
    value_grad_ref[...] = (value_weight * grad_bytes).astype(jnp.bfloat16)
    pairs = neighbours(jnp.broadcast_to(ids_ref[...], prob.shape))
    both = prob * prob_grad
    ahead, behind = over_patch(both, pairs, jnp.add, 0.0)
    score_grad = prob * (prob_grad - (ahead + (behind - both))) * SCALE
    weight = contract_rows(score_grad.astype(jnp.bfloat16), expand)
    query_bytes = contract_rows(member, query_ref[...])
    key_grad_ref[...] = (weight * query_bytes).astype(jnp.bfloat16)
    high, low = split_halves(weight * key_ref[...].astype(jnp.float32))
    query_grad = jnp.dot(member, high, preferred_element_type=jnp.float32) + jnp.dot(
        member, low, preferred_element_type=jnp.float32
    )
    query_grad_ref[...] = query_grad.astype(jnp.bfloat16)


def run_kernel(body, outs, *operands):
    vmem = pl.BlockSpec(memory_space=pltpu.VMEM)
    return pl.pallas_call(
        body,
        out_shape=outs,
        in_specs=[vmem] * len(operands),
        out_specs=[vmem] * len(outs),
        compiler_params=pltpu.CompilerParams(vmem_limit_bytes=VMEM_LIMIT),
        cost_estimate=pl.CostEstimate(
            flops=8_000_000_000, bytes_accessed=8_000_000, transcendentals=0
        ),
    )(*operands)


def local(byte_state, patch_id, w_query, w_key, w_value, w_out, out_grad):
    seq_rank = lax.axis_index("seq")
    model_rank = lax.axis_index("mp")
    n_model = lax.axis_size("mp")
    width = w_query.shape[1]
    half = width // 2
    heads = width // HEAD
    patch_rows = out_grad.shape[0]
    byte_rows = byte_state.shape[0]
    slots = -(-(patch_rows + DRIFT) // 128) * 128

    first = gather_rows(jnp.concatenate([w_key, w_query[:, :half]], axis=1), "seq", False)
    second = gather_rows(jnp.concatenate([w_value, w_query[:, half:]], axis=1), "seq", True)
    full_key, full_value = first[:, :width], second[:, :width]
    full_query = jnp.concatenate([first[:, width:], second[:, width:]], axis=1)

    group = min(2, lax.axis_size("seq").bit_length() - 1)
    out_half = w_out.shape[1] // 2
    full_out = jnp.concatenate(
        [
            gather_rows(after(w_out[:, :out_half], first), "seq", False),
            gather_rows(after(w_out[:, out_half:], second), "seq", True),
        ],
        axis=1,
    )
    steps = [list(range(group)), list(range(group))[::-1]]
    part = [after(out_grad[:, :out_half], full_out), after(out_grad[:, out_half:], full_out)]
    part = [gather_rows(p, "seq", False, s[:1]) for p, s in zip(part, steps)]
    shared = [
        gather_pair(p.reshape(2, patch_rows, out_half), "seq", s[0], s[1]) if group == 2 else p
        for p, s in zip(part, steps)
    ]
    group_out_grad = jnp.concatenate(shared, axis=1)

    first_patch = patch_id[0]
    last_patch = patch_id[byte_rows - 1]
    slot_index = jnp.arange(slots, dtype=jnp.int32)
    ids = (patch_id - first_patch)[None, :]
    member = ids == slot_index[:, None]
    member_half = member.astype(jnp.bfloat16)
    length = jnp.maximum(jnp.sum(member.astype(jnp.float32), axis=1), 1.0)
    pooled = (
        jnp.dot(member_half, byte_state, preferred_element_type=jnp.float32) / length[:, None]
    ).astype(jnp.bfloat16)

    keys = jnp.dot(byte_state, full_key, preferred_element_type=jnp.float32).astype(jnp.bfloat16)
    values = jnp.dot(byte_state, full_value, preferred_element_type=jnp.float32).astype(
        jnp.bfloat16
    )
    query_proj = jnp.dot(pooled, full_query, preferred_element_type=jnp.float32).astype(
        jnp.bfloat16
    )
    prob, attended = run_kernel(
        forward_kernel,
        [
            jax.ShapeDtypeStruct((heads, byte_rows), jnp.float32),
            jax.ShapeDtypeStruct((slots, width), jnp.bfloat16),
        ],
        ids, member_half, query_proj, keys, values,
    )

    target_row = first_patch - seq_rank * patch_rows + slot_index
    slot_live = slot_index <= last_patch - first_patch
    own_map = (
        (target_row[None, :] == jnp.arange(patch_rows, dtype=jnp.int32)[:, None])
        & slot_live[None, :]
    ).astype(jnp.bfloat16)
    next_map = (
        (target_row[None, :] - patch_rows == jnp.arange(DRIFT, dtype=jnp.int32)[:, None])
        & slot_live[None, :]
    ).astype(jnp.bfloat16)
    outgoing = jnp.dot(next_map, attended, preferred_element_type=jnp.float32).astype(jnp.bfloat16)
    incoming = passed_along(outgoing, "seq", 1)
    own_block = jnp.dot(own_map, attended, preferred_element_type=jnp.float32)
    own_block = (
        own_block + jnp.pad(incoming.astype(jnp.float32), ((0, patch_rows - DRIFT), (0, 0)))
    ).astype(jnp.bfloat16)
    if n_model == 2:
        other_block = swapped(own_block, "mp", 0)
        heads_all = jnp.concatenate(
            [
                jnp.where(model_rank == 0, own_block, other_block),
                jnp.where(model_rank == 0, other_block, own_block),
            ],
            axis=1,
        )
    else:
        heads_all = lax.all_gather(own_block, "mp", axis=1, tiled=True)
    group_heads = grouped_rows(grouped_columns(heads_all, "seq", group), "seq", group)
    grad_out = contract_rows(group_heads, group_out_grad)
    patch_embed = jnp.dot(heads_all, full_out, preferred_element_type=jnp.float32).astype(
        jnp.bfloat16
    )

    partial_sum = contract_cols(out_grad, full_out).astype(jnp.bfloat16)
    if n_model == 2:
        mine = lax.dynamic_slice_in_dim(partial_sum, model_rank * width, width, 1)
        theirs = lax.dynamic_slice_in_dim(partial_sum, (1 - model_rank) * width, width, 1)
        head_grad = (
            mine.astype(jnp.float32) + swapped(theirs, "mp", 0).astype(jnp.float32)
        ).astype(jnp.bfloat16)
    else:
        head_grad = lax.dynamic_slice_in_dim(
            lax.psum(partial_sum, "mp"), model_rank * width, width, 1
        )
    returned = passed_along(head_grad[:DRIFT], "seq", -1)
    slot_grad = (contract_rows(own_map, head_grad) + contract_rows(next_map, returned)).astype(
        jnp.bfloat16
    )
    key_grad, value_grad, query_grad = run_kernel(
        backward_kernel,
        [
            jax.ShapeDtypeStruct((byte_rows, width), jnp.bfloat16),
            jax.ShapeDtypeStruct((byte_rows, width), jnp.bfloat16),
            jax.ShapeDtypeStruct((slots, width), jnp.bfloat16),
        ],
        ids, member_half, query_proj, keys, values, prob, after(slot_grad, part),
    )
    grad_out = jnp.concatenate(
        [
            scatter_sum(grad_out[:, :out_half], "seq", False, group),
            scatter_sum(grad_out[:, out_half:], "seq", True, group),
        ],
        axis=1,
    )
    grad_key = scatter_sum(contract_rows(byte_state, key_grad), "seq", False)
    grad_value = scatter_sum(contract_rows(byte_state, value_grad), "seq", True)
    grad_query = contract_rows(pooled, query_grad)
    grad_query = jnp.concatenate(
        [
            scatter_sum(grad_query[:, :half], "seq", False),
            scatter_sum(grad_query[:, half:], "seq", True),
        ],
        axis=1,
    )
    pooled_grad = (contract_cols(query_grad, full_query) / length[:, None]).astype(jnp.bfloat16)
    byte_part = (
        contract_cols(key_grad, full_key)
        + contract_cols(value_grad, full_value)
        + contract_rows(member_half, pooled_grad)
    )
    byte_grad = pair_sum(byte_part.astype(jnp.bfloat16), "mp")
    return (patch_embed, byte_grad, grad_query, grad_key, grad_value, grad_out)


def solution(mesh):
    in_specs = (
        P("seq", None),
        P("seq"),
        P("seq", "mp"),
        P("seq", "mp"),
        P("seq", "mp"),
        P("seq", "mp"),
        P("seq", "mp"),
    )
    out_specs = (
        P("seq", "mp"),
        P("seq", None),
        P("seq", "mp"),
        P("seq", "mp"),
        P("seq", "mp"),
        P("seq", "mp"),
    )
    return jax.shard_map(local, mesh=mesh, in_specs=in_specs, out_specs=out_specs, check_vma=False)
```

```python
import jax
import jax.numpy as jnp
from jax import lax
from jax.experimental import pallas as pl
from jax.experimental.pallas import tpu as pltpu
from jax.sharding import PartitionSpec as P

HEAD = 64
DRIFT = 56
MAXLEN = 16
SCALE = HEAD ** (-0.5)
VMEM_LIMIT = 48 * 1024 * 1024


def passed_along(value, axis, steps):
    count = lax.axis_size(axis)
    initial, last = (max(0, -steps), min(count, count - steps))
    return lax.ppermute(value, axis, [(source, source + steps) for source in range(initial, last)])


def swapped(value, axis, bit):
    count = lax.axis_size(axis)
    return lax.ppermute(value, axis, [(i, i ^ (1 << bit)) for i in range(count)])


def contract_cols(left_side, right_side):
    return lax.dot_general(
        left_side, right_side, (((1,), (1,)), ((), ())), preferred_element_type=jnp.float32
    )


def contract_rows(left_side, right_side):
    return lax.dot_general(
        left_side, right_side, (((0,), (0,)), ((), ())), preferred_element_type=jnp.float32
    )


def bit_order(axis, flip, start=0):
    bits = lax.axis_size(axis).bit_length() - 1
    order = list(range(start, bits))
    if flip and len(order) > 1:
        order[0], order[1] = order[1], order[0]
    return order


def after(value, earlier):
    return lax.optimization_barrier((value, earlier))[0]


def scatter_sum(value, axis, flip, start=0, ties=None):
    rank = lax.axis_index(axis)
    order = bit_order(axis, flip, start)
    bits = len(order)
    value = value.reshape((2,) * bits + (value.shape[0] >> bits, value.shape[1]))
    left = sorted(order, reverse=True)
    for step, bit in enumerate(order):
        if ties and step in ties:
            value = after(value, ties[step])
        at = left.index(bit)
        mine = (rank >> bit) & 1
        send = lax.dynamic_index_in_dim(value, 1 - mine, at, keepdims=False)
        keep = lax.dynamic_index_in_dim(value, mine, at, keepdims=False)
        other = swapped(send, axis, bit)
        value = keep + other
        left.pop(at)
    return value


def gather_rows(value, axis, flip, ties=None):
    cols = value.shape[1]
    ties = ties or {}
    held, stages = [], []
    for step, bit in enumerate(reversed(bit_order(axis, flip))):
        if step in ties:
            value = after(value, ties[step])
        value = doubled(value, axis, held, bit)
        held.append(bit)
        stages.append(value)
    return stages + [value.reshape(-1, cols)]


def doubled(value, axis, held, bit):
    other = swapped(value, axis, bit)
    mine = ((lax.axis_index(axis) >> bit) & 1) == 0
    at = sum(1 for b in held if b > bit)
    return jnp.stack([jnp.where(mine, value, other), jnp.where(mine, other, value)], axis=at)


def grouped_columns(value, axis, group):
    width = value.shape[1]
    count = lax.axis_size(axis)
    block = width // count
    source = lax.broadcasted_iota(jnp.int32, (width, width), 0)
    place = lax.broadcasted_iota(jnp.int32, (width, width), 1)
    owner = (place % (width >> group)) // block << group
    for bit in range(group):
        owner = owner + ((place // (width >> (bit + 1))) % 2 << bit)
    chosen = (source == owner * block + place % block).astype(jnp.bfloat16)
    return jnp.dot(value, chosen, preferred_element_type=jnp.float32).astype(value.dtype)


def grouped_rows(value, axis, group):
    rank = lax.axis_index(axis)
    cols = value.shape[1]
    value = value[None]
    for bit in range(group):
        cols //= 2
        upper = ((rank >> bit) & 1) == 1
        low, high = value[:, :, :cols], value[:, :, cols:]
        keep, send = jnp.where(upper, high, low), jnp.where(upper, low, high)
        other = swapped(send, axis, bit)
        value = jnp.concatenate(
            [jnp.where(upper, other, keep), jnp.where(upper, keep, other)], axis=0
        )
    return value.reshape(-1, cols)


def pair_sum(value, axis):
    if lax.axis_size(axis) != 2:
        return lax.psum(value, axis)
    other = swapped(value, axis, 0)
    return (value.astype(jnp.float32) + other.astype(jnp.float32)).astype(value.dtype)


def split_halves(product):
    high = product.astype(jnp.bfloat16)
    low = (product - high.astype(jnp.float32)).astype(jnp.bfloat16)
    return high, low


def neighbours(ids):
    pairs = []
    count = ids.shape[1]
    where_at = lax.broadcasted_iota(jnp.int32, ids.shape, 1)
    step = 1
    while step < MAXLEN:
        before = (pltpu.roll(ids, step, 1) == ids) & (where_at >= step)
        after = (pltpu.roll(ids, count - step, 1) == ids) & (where_at < count - step)
        pairs.append((step, before, after))
        step *= 2
    return pairs


def over_patch(value, pairs, combine, neutral):
    count = value.shape[1]
    ahead = behind = value
    for step, before, after in pairs:
        ahead = combine(ahead, jnp.where(before, pltpu.roll(ahead, step, 1), neutral))
        behind = combine(behind, jnp.where(after, pltpu.roll(behind, count - step, 1), neutral))
    return ahead, behind


def head_rows(heads, width):
    row = lax.broadcasted_iota(jnp.int32, (heads, width), 0)
    col = lax.broadcasted_iota(jnp.int32, (heads, width), 1)
    return ((col >= row * HEAD) & (col < row * HEAD + HEAD)).astype(jnp.float32).astype(jnp.bfloat16)


def forward_kernel(ids_ref, member_ref, query_ref, key_ref, value_ref, prob_ref, attended_ref):
    heads, width = prob_ref.shape[0], query_ref.shape[1]
    member = member_ref[...]
    expand = head_rows(heads, width)
    query_bytes = contract_rows(member, query_ref[...])
    high, low = split_halves(query_bytes * key_ref[...].astype(jnp.float32))
    scores = (contract_cols(expand, high) + contract_cols(expand, low)) * SCALE
    pairs = neighbours(jnp.broadcast_to(ids_ref[...], scores.shape))
    peak = jnp.maximum(*over_patch(scores, pairs, jnp.maximum, -1e30))
    terms = jnp.exp(scores - peak)
    ahead, behind = over_patch(terms, pairs, jnp.add, 0.0)
    prob = terms / (ahead + (behind - terms))
    prob_ref[...] = prob
    weight = contract_rows(prob.astype(jnp.bfloat16), expand)
    high, low = split_halves(weight * value_ref[...].astype(jnp.float32))
    attended = jnp.dot(member, high, preferred_element_type=jnp.float32) + jnp.dot(
        member, low, preferred_element_type=jnp.float32
    )
    attended_ref[...] = attended.astype(jnp.bfloat16)


def backward_kernel(
    ids_ref, member_ref, query_ref, key_ref, value_ref, prob_ref, grad_ref,
    key_grad_ref, value_grad_ref, query_grad_ref,
):
    heads, width = prob_ref.shape[0], query_ref.shape[1]
    member = member_ref[...]
    expand = head_rows(heads, width)
    prob = prob_ref[...]
    grad_bytes = contract_rows(member, grad_ref[...])
    high, low = split_halves(grad_bytes * value_ref[...].astype(jnp.float32))
    prob_grad = contract_cols(expand, high) + contract_cols(expand, low)
    value_weight = contract_rows(prob.astype(jnp.bfloat16), expand)
    value_grad_ref[...] = (value_weight * grad_bytes).astype(jnp.bfloat16)
    pairs = neighbours(jnp.broadcast_to(ids_ref[...], prob.shape))
    both = prob * prob_grad
    ahead, behind = over_patch(both, pairs, jnp.add, 0.0)
    score_grad = prob * (prob_grad - (ahead + (behind - both))) * SCALE
    weight = contract_rows(score_grad.astype(jnp.bfloat16), expand)
    query_bytes = contract_rows(member, query_ref[...])
    key_grad_ref[...] = (weight * query_bytes).astype(jnp.bfloat16)
    high, low = split_halves(weight * key_ref[...].astype(jnp.float32))
    query_grad = jnp.dot(member, high, preferred_element_type=jnp.float32) + jnp.dot(
        member, low, preferred_element_type=jnp.float32
    )
    query_grad_ref[...] = query_grad.astype(jnp.bfloat16)


def run_kernel(body, outs, *operands):
    vmem = pl.BlockSpec(memory_space=pltpu.VMEM)
    return pl.pallas_call(
        body,
        out_shape=outs,
        in_specs=[vmem] * len(operands),
        out_specs=[vmem] * len(outs),
        compiler_params=pltpu.CompilerParams(vmem_limit_bytes=VMEM_LIMIT),
        cost_estimate=pl.CostEstimate(
            flops=8_000_000_000, bytes_accessed=8_000_000, transcendentals=0
        ),
    )(*operands)


def local(byte_state, patch_id, w_query, w_key, w_value, w_out, out_grad):
    seq_rank = lax.axis_index("seq")
    model_rank = lax.axis_index("mp")
    n_model = lax.axis_size("mp")
    width = w_query.shape[1]
    half = width // 2
    heads = width // HEAD
    patch_rows = out_grad.shape[0]
    byte_rows = byte_state.shape[0]
    slots = -(-(patch_rows + DRIFT) // 128) * 128

    steps = lax.axis_size("seq").bit_length() - 1
    group = min(2, steps)
    rest = steps - group
    out_half = w_out.shape[1] // 2
    shared = [out_grad[:, :out_half], out_grad[:, out_half:]]
    ties = {}
    held = []
    for step in range(group):
        bits = [step, group - 1 - step]
        shared = [doubled(value, "seq", [h[i] for h in held], bits[i]) for i, value in enumerate(shared)]
        held.append(bits)
        ties[rest + step] = list(shared)
    group_out_grad = jnp.concatenate([value.reshape(-1, out_half) for value in shared], axis=1)
    first = gather_rows(
        jnp.concatenate([w_key, w_query[:, :half]], axis=1), "seq", False, ties
    )
    second = gather_rows(
        jnp.concatenate([w_value, w_query[:, half:]], axis=1), "seq", True, ties
    )
    ties = {rest: [first[-1], second[-1]]}
    if rest:
        ties[0] = [first[rest - 1], second[rest - 1]]
    first, second = first[-1], second[-1]
    full_out = jnp.concatenate(
        [
            gather_rows(w_out[:, :out_half], "seq", False, ties)[-1],
            gather_rows(w_out[:, out_half:], "seq", True, ties)[-1],
        ],
        axis=1,
    )
    full_key, full_value = first[:, :width], second[:, :width]
    full_query = jnp.concatenate([first[:, width:], second[:, width:]], axis=1)

    first_patch = patch_id[0]
    last_patch = patch_id[byte_rows - 1]
    slot_index = jnp.arange(slots, dtype=jnp.int32)
    ids = (patch_id - first_patch)[None, :]
    member = ids == slot_index[:, None]
    member_half = member.astype(jnp.bfloat16)
    length = jnp.maximum(jnp.sum(member.astype(jnp.float32), axis=1), 1.0)
    pooled = (
        jnp.dot(member_half, byte_state, preferred_element_type=jnp.float32) / length[:, None]
    ).astype(jnp.bfloat16)

    keys = jnp.dot(byte_state, full_key, preferred_element_type=jnp.float32).astype(jnp.bfloat16)
    values = jnp.dot(byte_state, full_value, preferred_element_type=jnp.float32).astype(
        jnp.bfloat16
    )
    query_proj = jnp.dot(pooled, full_query, preferred_element_type=jnp.float32).astype(
        jnp.bfloat16
    )
    prob, attended = run_kernel(
        forward_kernel,
        [
            jax.ShapeDtypeStruct((heads, byte_rows), jnp.float32),
            jax.ShapeDtypeStruct((slots, width), jnp.bfloat16),
        ],
        ids, member_half, query_proj, keys, values,
    )

    target_row = first_patch - seq_rank * patch_rows + slot_index
    slot_live = slot_index <= last_patch - first_patch
    own_map = (
        (target_row[None, :] == jnp.arange(patch_rows, dtype=jnp.int32)[:, None])
        & slot_live[None, :]
    ).astype(jnp.bfloat16)
    next_map = (
        (target_row[None, :] - patch_rows == jnp.arange(DRIFT, dtype=jnp.int32)[:, None])
        & slot_live[None, :]
    ).astype(jnp.bfloat16)
    outgoing = jnp.dot(next_map, attended, preferred_element_type=jnp.float32).astype(jnp.bfloat16)
    incoming = passed_along(outgoing, "seq", 1)
    own_block = jnp.dot(own_map, attended, preferred_element_type=jnp.float32)
    own_block = (
        own_block + jnp.pad(incoming.astype(jnp.float32), ((0, patch_rows - DRIFT), (0, 0)))
    ).astype(jnp.bfloat16)
    if n_model == 2:
        other_block = swapped(own_block, "mp", 0)
        heads_all = jnp.concatenate(
            [
                jnp.where(model_rank == 0, own_block, other_block),
                jnp.where(model_rank == 0, other_block, own_block),
            ],
            axis=1,
        )
    else:
        heads_all = lax.all_gather(own_block, "mp", axis=1, tiled=True)
    group_heads = grouped_rows(grouped_columns(heads_all, "seq", group), "seq", group)
    grad_out = contract_rows(group_heads, group_out_grad)
    patch_embed = jnp.dot(heads_all, full_out, preferred_element_type=jnp.float32).astype(
        jnp.bfloat16
    )

    partial_sum = contract_cols(out_grad, full_out).astype(jnp.bfloat16)
    if n_model == 2:
        mine = lax.dynamic_slice_in_dim(partial_sum, model_rank * width, width, 1)
        theirs = lax.dynamic_slice_in_dim(partial_sum, (1 - model_rank) * width, width, 1)
        head_grad = (
            mine.astype(jnp.float32) + swapped(theirs, "mp", 0).astype(jnp.float32)
        ).astype(jnp.bfloat16)
    else:
        head_grad = lax.dynamic_slice_in_dim(
            lax.psum(partial_sum, "mp"), model_rank * width, width, 1
        )
    returned = passed_along(head_grad[:DRIFT], "seq", -1)
    slot_grad = (contract_rows(own_map, head_grad) + contract_rows(next_map, returned)).astype(
        jnp.bfloat16
    )
    key_grad, value_grad, query_grad = run_kernel(
        backward_kernel,
        [
            jax.ShapeDtypeStruct((byte_rows, width), jnp.bfloat16),
            jax.ShapeDtypeStruct((byte_rows, width), jnp.bfloat16),
            jax.ShapeDtypeStruct((slots, width), jnp.bfloat16),
        ],
        ids, member_half, query_proj, keys, values, prob, after(slot_grad, grad_out),
    )
    grad_out = jnp.concatenate(
        [
            scatter_sum(grad_out[:, :out_half], "seq", False, group),
            scatter_sum(grad_out[:, out_half:], "seq", True, group),
        ],
        axis=1,
    )
    grad_first = jnp.concatenate(
        [contract_rows(byte_state, key_grad), contract_rows(pooled, query_grad[:, :half])], axis=1
    )
    grad_second = jnp.concatenate(
        [contract_rows(byte_state, value_grad), contract_rows(pooled, query_grad[:, half:])],
        axis=1,
    )
    key_grad, value_grad, query_grad = lax.optimization_barrier(
        (key_grad, value_grad, query_grad, grad_first, grad_second)
    )[:3]
    ties = {group: grad_out}
    grad_first = scatter_sum(grad_first, "seq", False, 0, ties)
    grad_second = scatter_sum(grad_second, "seq", True, 0, ties)
    grad_key, grad_value = grad_first[:, :width], grad_second[:, :width]
    grad_query = jnp.concatenate([grad_first[:, width:], grad_second[:, width:]], axis=1)
    pooled_grad = (contract_cols(query_grad, full_query) / length[:, None]).astype(jnp.bfloat16)
    byte_part = (
        contract_cols(key_grad, full_key)
        + contract_cols(value_grad, full_value)
        + contract_rows(member_half, pooled_grad)
    )
    byte_grad = pair_sum(byte_part.astype(jnp.bfloat16), "mp")
    return (patch_embed, byte_grad, grad_query, grad_key, grad_value, grad_out)


def solution(mesh):
    in_specs = (
        P("seq", None),
        P("seq"),
        P("seq", "mp"),
        P("seq", "mp"),
        P("seq", "mp"),
        P("seq", "mp"),
        P("seq", "mp"),
    )
    out_specs = (
        P("seq", "mp"),
        P("seq", None),
        P("seq", "mp"),
        P("seq", "mp"),
        P("seq", "mp"),
        P("seq", "mp"),
    )
    return jax.shard_map(local, mesh=mesh, in_specs=in_specs, out_specs=out_specs, check_vma=False)
```
